256 devices in a mesh: chan: 64 (over x_hi, y, z), seg: 4 (over x_lo, core).
Axes of the slice: x: 4 (x_hi: 2, x_lo: 2; x = x_hi * 2 + x_lo), y: 4, z: 8, core: 2. Of those that a mesh axis runs over, the one named last changes fastest.
Arguments:
- spectra: bfloat16 [2, 256, 2048, 256], P(None, 'seg', 'chan'), may hold values from -6 to 6
- pair_bins: int32 [64, 64, 1], P('chan'), may hold values from 0 to 127; in each aligned block of 64 rows (0 to 63, 64 to 127, ..., all dimensions but the last counted through in order) at most 2 rows name the same one
Outputs:
- offset_gathers: float32 [128, 256], P('chan', 'seg')
The draws below stay inside these ranges and needn't reach their ends.
Inputs may be any that keep to these rules, and one draw needn't show every extreme that they name: `pair_bins`: in the 64 rows of one source block no bin is named more than 2 times; every bin is named by some row.
All inputs are finite; a program needn't handle non-finite values.
Results may differ from the reference program's by a relative error of at most 0.0003.
Values may be sent and summed in bfloat16 or wider, within the bound.
A program may use at most 64 MiB of HBM per device.

```python
import math
import jax
import jax.numpy as jnp
import numpy as np
from jax import lax

CHAN_DEV = 32
FREQ = 256
LAGS = 256
NFFT = 1024
LOW_BIN = 16
BIN_WIDTH = 4
REACH = 3
BIN_DEV = 2
PANELS = 64
NBINS = 128
MOST = 2
CHANNELS = 2048
WINDOWS = 256
N_CHAN = 64


def block_levels(rng, dims, split, smallest, top_value):
    gain, own = 1.0, jax.random.fold_in(rng, 6)
    for dim, parts in split:
        heights = jnp.exp(jax.random.uniform(jax.random.fold_in(own, dim), (parts,), jnp.float32, smallest / len(split), top_value / len(split)))
        gain = gain * jnp.repeat(heights, dims[dim] // parts).reshape([-1 if axis == dim else 1 for axis in range(len(dims))])
    return gain


def routed_block(stream_key, own, number, rows, amount, top, most, slope):
    sequence = jax.random.permutation(stream_key, amount)
    heavy_load, common = load_shares(amount, rows * top, most, slope, True), load_shares(amount, rows * top, most, slope, False)
    places = jnp.arange(amount)

    def named(lengths, turn):
        used = int((lengths > 0).sum())
        fixed = max(1, used // 4)
        passed = fixed + (places - fixed + turn * (used - fixed)) % max(1, amount - fixed)
        return jnp.zeros((amount,), jnp.int32).at[sequence[jnp.where(places < fixed, places, passed)]].set(jnp.asarray(lengths, jnp.int32))

    lengths = jnp.where(number % 4 == 0, named(heavy_load, number // 4), named(common, number - number // 4 - 1))
    mixed = jax.random.permutation(jax.random.fold_in(own, 3), amount)
    giver, sink = mixed[0:amount // 2 * 2:2], mixed[1:amount // 2 * 2:2]
    room = jnp.minimum(lengths[giver] - 1, most - lengths[sink]) // 2
    room = jnp.where((giver == sequence[0]) | (sink == sequence[0]) | (lengths[sink] == 0), 0, jnp.maximum(room, 0))
    passed = jax.random.randint(jax.random.fold_in(own, 4), (amount // 2,), 0, 1 << 20) % (room + 1)
    lengths = lengths.at[giver].add(-passed).at[sink].add(passed)
    members = jnp.searchsorted(jnp.cumsum(lengths), jnp.arange(rows * top), side="right").astype(jnp.int32)
    table = members.reshape(top, rows).T
    table = table[jax.random.permutation(jax.random.fold_in(own, 1), rows)]
    turn = jax.random.randint(jax.random.fold_in(own, 2), (rows, 1), 0, top)
    return jnp.take_along_axis(table, (jnp.arange(top)[None, :] + turn) % top, axis=1)


def load_shares(number_of, total, reach, lean, full):
    weights = [(1 << 20) // math.isqrt(standing ** lean) + 1 for standing in range(1, number_of + 1)]
    largest = reach if full else min(reach, max(-(-total // number_of), total * weights[0] // sum(weights)))
    least = 1 if total - largest >= number_of - 1 else 0
    holding, rest = [largest] + [least] * (number_of - 1), total - largest - least * (number_of - 1)
    while rest > 0:
        movable = [i for i in range(1, number_of) if holding[i] < largest] or [i for i in range(1, number_of) if holding[i] < reach]
        whole, budget = sum([weights[i] for i in movable]), rest
        for i in movable:
            extra = min(reach - holding[i], max(1, budget * weights[i] // whole), rest)
            holding[i] = holding[i] + extra
            rest = rest - extra
    return np.array(holding)


def centred(own_key, shape, width, reach, split=(), kind=jnp.bfloat16):
    values = width * jax.random.normal(own_key, shape, jnp.float32)
    if split:
        values = values * block_levels(own_key, shape, split, -0.22, 0.18)
    return jnp.clip(values, -reach, reach).astype(kind)


def setup_inputs(seed: int = 0) -> dict:
    seeds = jax.random.split(jax.random.key(seed), 3)
    spectra = centred(seeds[0], (2, WINDOWS, CHANNELS, FREQ), 1.0, 6.0, ((1, 4), (2, 64)))
    pair_bins_keys = jax.random.split(jax.random.fold_in(seeds[1], 1), N_CHAN * PANELS // PANELS)
    pair_bins_turns = jax.random.permutation(jax.random.fold_in(seeds[1], 3), N_CHAN * PANELS // PANELS)
    pair_bins = jax.vmap(lambda own, number: routed_block(jax.random.fold_in(seeds[1], 2), own, number, PANELS, NBINS, 1, MOST, 2))(pair_bins_keys, pair_bins_turns).reshape((N_CHAN, PANELS, 1))
    return dict(spectra=spectra, pair_bins=pair_bins)


def lag_table(freq_count, lag_count):
    bin_index = jnp.arange(freq_count, dtype=jnp.int32) + LOW_BIN
    lag_index = jnp.arange(lag_count, dtype=jnp.int32) - lag_count // 2
    phase = bin_index[:, None] * lag_index[None, :] % NFFT
    theta = phase.astype(jnp.float32) * (2.0 * math.pi / NFFT)
    return jnp.concatenate([jnp.cos(theta), -jnp.sin(theta)], axis=0)

def panel_sums(cross_block, same_block):
    components = cross_block.shape[0]
    freq_count = cross_block.shape[1]
    block_width = cross_block.shape[2]
    flipped = cross_block[:, :, ::-1, :]
    padded = jnp.pad(flipped, ((0, 0), (0, 0), (0, 0), (0, block_width)))
    flattened = padded.reshape(components, freq_count, 2 * block_width * block_width)
    flattened = flattened[:, :, :block_width * (2 * block_width - 1)]
    skewed = flattened.reshape(components, freq_count, block_width, 2 * block_width - 1)
    diagonals = jnp.pad(lax.optimization_barrier(jnp.sum(skewed, axis=2)), ((0, 0), (0, 0), (1, 0)))
    if same_block:
        keep_mask = (jnp.arange(2 * block_width) != block_width).astype(diagonals.dtype)
        diagonals = diagonals * keep_mask
    grouped = diagonals.reshape(components, freq_count, 2 * block_width // BIN_WIDTH, BIN_WIDTH).sum(axis=3)
    return jnp.transpose(grouped, (2, 0, 1)).reshape(grouped.shape[2], components * freq_count)

def cross_block(source_block, partner_block):
    real_a = source_block[0].astype(jnp.float32)
    imag_a = source_block[1].astype(jnp.float32)
    real_b = partner_block[0].astype(jnp.float32)
    imag_b = partner_block[1].astype(jnp.float32)
    real_part = jnp.einsum('wah,wbh->hab', real_a, real_b) + jnp.einsum('wah,wbh->hab', imag_a, imag_b)
    imag_part = jnp.einsum('wah,wbh->hab', real_a, imag_b) - jnp.einsum('wah,wbh->hab', imag_a, real_b)
    return jnp.stack([real_part, imag_part])

def reference(spectra, pair_bins):
    blocks = spectra.reshape(2, WINDOWS, N_CHAN, CHAN_DEV, FREQ)

    def one_source(source):
        source_block = lax.dynamic_index_in_dim(blocks, source, 2, keepdims=False)
        panel_list = []
        for offset in range(REACH + 1):
            partner = jnp.maximum(source - offset, 0).astype(jnp.int32)
            partner_block = lax.dynamic_index_in_dim(blocks, partner, 2, keepdims=False)
            present = (source - offset >= 0).astype(jnp.float32)
            panel_list.append(panel_sums(cross_block(source_block, partner_block), offset == 0) * present)
        return jnp.concatenate(panel_list, axis=0)
    spectral = lax.map(one_source, jnp.arange(N_CHAN, dtype=jnp.int32))
    transform = lag_table(FREQ, LAGS)
    lagged = jnp.dot(spectral.reshape(N_CHAN * PANELS, 2 * FREQ), transform, precision=lax.Precision.HIGHEST)
    stacked = jax.ops.segment_sum(lagged, pair_bins.reshape(N_CHAN * PANELS), num_segments=NBINS)
    norm_factor = 1.0 / math.sqrt(WINDOWS * CHAN_DEV * BIN_WIDTH * FREQ * PANELS / BIN_DEV)
    return stacked * norm_factor
```

```python
import functools
import math

import jax
import jax.numpy as jnp
import numpy as np
from jax import lax
from jax.experimental import pallas as pl
from jax.experimental.pallas import tpu as pltpu
from jax.sharding import PartitionSpec as P

LAGS = 256
NFFT = 1024
LOW_BIN = 16
BIN_WIDTH = 4
REACH = 3
BIN_DEV = 2

MESH = pl.DeviceIdType.MESH
RING = 8
ROWS = 8
SEGS = 4
BLOCK = 32
PANELS = 64
HALO = REACH
CHUNKS = 4
F32 = jnp.float32
BF16 = jnp.bfloat16


def lag_table(freq_count, lag_count):
    bin_index = np.arange(freq_count, dtype=np.int64) + LOW_BIN
    lag_index = np.arange(lag_count, dtype=np.int64) - lag_count // 2
    phase = bin_index[:, None] * lag_index[None, :] % NFFT
    theta = phase.astype(np.float64) * (2.0 * math.pi / NFFT)
    return np.concatenate([np.cos(theta), -np.sin(theta)], axis=0).astype(np.float32)


def split_two(value):
    high = value.astype(BF16)
    return high, (value - high.astype(F32)).astype(BF16)


def kernel(
    norm_factor, x_ref, pb_ref, table_ref, o_ref,
    gathered, sources, sums, totals, panels, bins_in, stage_out, stage_in, last_out, last_in,
    local_sem, x_send, x_recv, h_send, h_recv, b_send, b_recv, s_send, s_recv, l_send, l_recv,
):
    chan = lax.axis_index("chan")
    seg = lax.axis_index("seg")
    z = lax.rem(chan, RING)
    row = lax.div(chan, RING)
    base = chan - z
    mine = row * SEGS + seg
    width = RING // CHUNKS

    def ring_peer(d):
        return lax.rem(z + d, RING)

    next_row = lax.rem(row + 1, ROWS) * RING + z
    prev_row = lax.rem(row + ROWS - 1, ROWS) * RING + z

    barrier = pltpu.get_barrier_semaphore()
    for d in range(1, RING):
        pl.semaphore_signal(barrier, inc=1, device_id=(base + ring_peer(d), seg), device_id_type=MESH)
    pl.semaphore_signal(barrier, inc=1, device_id=(next_row, seg), device_id_type=MESH)
    pl.semaphore_signal(barrier, inc=1, device_id=(prev_row, seg), device_id_type=MESH)

    def greet(d, carry):
        other = lax.rem(mine + d, ROWS * SEGS)
        pl.semaphore_signal(
            barrier, inc=1,
            device_id=(lax.div(other, SEGS) * RING + z, lax.rem(other, SEGS)), device_id_type=MESH,
        )
        return carry

    lax.fori_loop(1, ROWS * SEGS, greet, 0)
    own = pltpu.make_async_copy(x_ref.at[:, pl.ds(z * RING, RING)], gathered.at[HALO + z], local_sem.at[0])
    own.start()
    own_bins = pltpu.make_async_copy(pb_ref, bins_in.at[z], local_sem.at[1])
    own_bins.start()
    pl.semaphore_wait(barrier, RING - 1 + 2 + ROWS * SEGS - 1)

    order = [4, 3, 5, 2, 6, 1, 7]

    def block_copy(chunk, d):
        to = ring_peer(d)
        return pltpu.make_async_remote_copy(
            src_ref=x_ref.at[:, pl.ds(to * RING + chunk * width, width)],
            dst_ref=gathered.at[HALO + z, :, pl.ds(chunk * width, width)],
            send_sem=x_send.at[chunk, d], recv_sem=x_recv.at[chunk, d],
            device_id=(base + to, seg), device_id_type=MESH,
        )

    def halo_copy(chunk):
        return pltpu.make_async_remote_copy(
            src_ref=gathered.at[pl.ds(RING, HALO), :, pl.ds(chunk * width, width)],
            dst_ref=gathered.at[pl.ds(0, HALO), :, pl.ds(chunk * width, width)],
            send_sem=h_send.at[chunk], recv_sem=h_recv.at[chunk],
            device_id=(next_row, seg), device_id_type=MESH,
        )

    def bins_copy(d):
        return pltpu.make_async_remote_copy(
            src_ref=pb_ref, dst_ref=bins_in.at[z],
            send_sem=b_send.at[d], recv_sem=b_recv.at[d],
            device_id=(base + ring_peer(d), seg), device_id_type=MESH,
        )

    for chunk in range(min(2, CHUNKS)):
        for d in order:
            block_copy(chunk, d).start()
    for d in order:
        bins_copy(d).start()

    def clear(n, carry):
        totals[n] = jnp.zeros(totals.shape[1:], F32)
        return carry

    lax.fori_loop(0, totals.shape[0], clear, 0)
    own.wait()
    own_bins.wait()

    def prepare(chunk, n, is_source):
        for w in range(width):
            for tile in range(2):
                lanes = pl.ds(tile * 128, 128)
                real = gathered[n, 0, chunk * width + w, :, lanes].astype(F32)
                imag = gathered[n, 1, chunk * width + w, :, lanes].astype(F32)
                if is_source:
                    sources[n - HALO, w, 0, tile] = real
                    sources[n - HALO, w, 1, tile] = imag
                    sources[n - HALO, w, 2, tile] = real - imag
                parts = []
                for part in (real, imag):
                    padded = jnp.concatenate([jnp.zeros((8, 128), F32), part], axis=0)
                    pairs = padded + pltpu.roll(padded, BLOCK + 8 - 1, 0)
                    parts.append((padded, pairs + pltpu.roll(pairs, BLOCK + 8 - 2, 0)))
                (real_pad, real_sum), (imag_pad, imag_sum) = parts
                odd_real = pltpu.roll(real_sum, BLOCK + 8 - 4, 0)
                odd_imag = pltpu.roll(imag_sum, BLOCK + 8 - 4, 0)
                sums[n, w, 0, 0, tile] = real_sum
                sums[n, w, 0, 1, tile] = imag_sum
                sums[n, w, 0, 2, tile] = real_sum + imag_sum
                sums[n, w, 1, 0, tile] = odd_real
                sums[n, w, 1, 1, tile] = odd_imag
                sums[n, w, 1, 2, tile] = odd_real + odd_imag
                if is_source:
                    other_real = real_sum - real_pad
                    other_imag = imag_sum - imag_pad
                    sums[n + RING, w, 0, 0, tile] = other_real
                    sums[n + RING, w, 0, 1, tile] = other_imag
                    sums[n + RING, w, 0, 2, tile] = other_real + other_imag

    def correlate(s, k):
        partner = HALO + s - k
        centre = jnp.where(k == 0, HALO + RING + s, partner)
        for tile in range(2):
            for parity in range(2):
                place = (s * (REACH + 1) + k) * 4 + tile * 2 + parity
                acc = [[totals[place, q * 3 + m] for m in range(3)] for q in range(8)]
                for w in range(width):
                    left = [[sources[s, w, m, tile, 8 * i:8 * i + 8, :] for m in range(3)] for i in range(4)]
                    for j in range(-1, 4):
                        at = slice(8 * j + 8, 8 * j + 16)
                        right = [sums[partner, w, parity, m, tile, at, :] for m in range(3)]
                        for i in range(4):
                            q = j - i + 4
                            if not 0 <= q < 8:
                                continue
                            used = right
                            if parity == 0 and q == 4:
                                used = [sums[centre, w, 0, m, tile, at, :] for m in range(3)]
                            for m in range(3):
                                acc[q][m] = acc[q][m] + left[i][m] * used[m]
                for q in range(8):
                    for m in range(3):
                        totals[place, q * 3 + m] = acc[q][m]

    def one_chunk(chunk, carry):
        for d in order:
            block_copy(chunk, d).wait_recv()
        halo_copy(chunk).start()
        for d in order:
            block_copy(chunk, d).wait_send()

        @pl.when(chunk + 2 < CHUNKS)
        def _():
            for d in order:
                block_copy(chunk + 2, d).start()

        def ready(n, c):
            prepare(chunk, n, True)
            return c

        lax.fori_loop(HALO, HALO + RING, ready, 0)

        def inner(n, c):
            correlate(lax.div(n, REACH + 1), lax.rem(n, REACH + 1))
            return c

        lax.fori_loop(REACH * (REACH + 1), RING * (REACH + 1), inner, 0)
        halo_copy(chunk).wait_recv()

        def ready_halo(n, c):
            prepare(chunk, n, False)
            return c

        lax.fori_loop(0, HALO, ready_halo, 0)
        lax.fori_loop(0, REACH * (REACH + 1), inner, 0)
        halo_copy(chunk).wait_send()
        return carry

    lax.fori_loop(0, CHUNKS, one_chunk, 0)

    def finish(n, carry):
        s = lax.div(n, REACH + 1)
        k = lax.rem(n, REACH + 1)
        present = jnp.where((row > 0) | (s >= k), 1.0, 0.0).astype(F32)
        for tile in range(2):
            for parity in range(2):
                place = n * 4 + tile * 2 + parity
                real, imag = [], []
                for q in range(8):
                    a, b, c = (totals[place, q * 3 + m] for m in range(3))
                    real.append(jnp.sum(a + b, axis=0, keepdims=True))
                    imag.append(jnp.sum(c - a + b, axis=0, keepdims=True))
                where = pl.ds(n * 16 + parity * 8, 8)
                panels[where, tile * 128:tile * 128 + 128] = jnp.concatenate(real, axis=0) * present
                panels[where, 256 + tile * 128:256 + tile * 128 + 128] = jnp.concatenate(imag, axis=0) * present
        return carry

    lax.fori_loop(0, RING * (REACH + 1), finish, 0)

    for d in order:
        bins_copy(d).wait()

    index = lax.broadcasted_iota(jnp.int32, (128, PANELS), 0)
    owner_z = lax.div(index, 16)
    bin_ids = 2 * (lax.rem(index, 8) * RING + owner_z) + lax.rem(lax.div(index, 8), 2)
    binned = jnp.zeros((128, 512), F32)
    for s in range(RING):
        hot = jnp.where(bin_ids == bins_in[s, :, 0:PANELS], 1.0, 0.0).astype(BF16)
        for part in split_two(panels[s * PANELS:(s + 1) * PANELS, :]):
            binned = binned + jnp.dot(hot, part, preferred_element_type=F32)
    high, low = split_two(binned)
    table_high, table_low = split_two(table_ref[...])
    lagged = (
        jnp.dot(high, table_high, preferred_element_type=F32)
        + jnp.dot(low, table_high, preferred_element_type=F32)
        + jnp.dot(high, table_low, preferred_element_type=F32)
    )
    stage_out[...] = lagged.reshape(RING, 16, LAGS)

    def stage_copy(d):
        to = ring_peer(d)
        return pltpu.make_async_remote_copy(
            src_ref=stage_out.at[to], dst_ref=stage_in.at[z],
            send_sem=s_send.at[d], recv_sem=s_recv.at[d],
            device_id=(base + to, seg), device_id_type=MESH,
        )

    for d in order:
        stage_copy(d).start()
    own_part = stage_out[z]
    for d in order:
        stage_copy(d).wait_recv()
    summed = own_part
    for d in range(1, RING):
        summed = summed + stage_in[ring_peer(d)]
    for g in range(SEGS):
        both = jnp.concatenate([summed[0:8, g * 64:g * 64 + 64], summed[8:16, g * 64:g * 64 + 64]], axis=1)
        for r in range(ROWS):
            last_out[r * SEGS + g] = both[r:r + 1, :]

    def last_copy(d):
        other = lax.rem(mine + d, ROWS * SEGS)
        return pltpu.make_async_remote_copy(
            src_ref=last_out.at[other], dst_ref=last_in.at[mine],
            send_sem=l_send.at[d], recv_sem=l_recv.at[d],
            device_id=(lax.div(other, SEGS) * RING + z, lax.rem(other, SEGS)), device_id_type=MESH,
        )

    def last_start(d, carry):
        last_copy(d).start()
        return carry

    def last_wait(d, carry):
        last_copy(d).wait_recv()
        return carry

    def last_sent(d, carry):
        last_copy(d).wait_send()
        return carry

    lax.fori_loop(1, ROWS * SEGS, last_start, 0)
    for d in order:
        stage_copy(d).wait_send()
    result = last_out[mine]
    lax.fori_loop(1, ROWS * SEGS, last_wait, 0)
    for d in range(1, ROWS * SEGS):
        result = result + last_in[lax.rem(mine + d, ROWS * SEGS)]
    result = result * norm_factor
    o_ref[0:1, :] = result[:, 0:64]
    o_ref[1:2, :] = result[:, 64:128]
    lax.fori_loop(1, ROWS * SEGS, last_sent, 0)


def on_device(spectra, pair_bins):
    window_count = spectra.shape[1]
    freq_count = spectra.shape[3]
    panel_count = pair_bins.shape[1]
    norm_factor = 1.0 / math.sqrt(
        window_count * SEGS * BLOCK * BIN_WIDTH * freq_count * panel_count / BIN_DEV
    )
    ids = pair_bins.reshape(REACH + 1, 8, 2).transpose(0, 2, 1).reshape(1, panel_count)
    ids = jnp.pad(ids, ((0, 0), (0, 128 - panel_count)))
    table = jnp.asarray(lag_table(freq_count, LAGS))
    width = RING // CHUNKS
    vmem = pl.BlockSpec(memory_space=pltpu.VMEM)
    dma = pltpu.SemaphoreType.DMA
    return pl.pallas_call(
        functools.partial(kernel, norm_factor),
        out_shape=jax.ShapeDtypeStruct((BIN_DEV, LAGS // SEGS), F32),
        in_specs=[pl.BlockSpec(memory_space=pl.ANY), vmem, vmem],
        out_specs=vmem,
        scratch_shapes=[
            pltpu.VMEM((HALO + RING, 2, RING, BLOCK, 256), BF16),
            pltpu.VMEM((RING, width, 3, 2, BLOCK, 128), F32),
            pltpu.VMEM((HALO + 2 * RING, width, 2, 3, 2, BLOCK + 8, 128), F32),
            pltpu.VMEM((RING * (REACH + 1) * 4, 24, 8, 128), F32),
            pltpu.VMEM((RING * PANELS, 512), F32),
            pltpu.VMEM((RING, 1, 128), jnp.int32),
            pltpu.VMEM((RING, 16, LAGS), F32),
            pltpu.VMEM((RING, 16, LAGS), F32),
            pltpu.VMEM((ROWS * SEGS, 1, 128), F32),
            pltpu.VMEM((ROWS * SEGS, 1, 128), F32),
            dma((2,)),
            dma((CHUNKS, RING)), dma((CHUNKS, RING)),
            dma((CHUNKS,)), dma((CHUNKS,)),
            dma((RING,)), dma((RING,)),
            dma((RING,)), dma((RING,)),
            dma((ROWS * SEGS,)), dma((ROWS * SEGS,)),
        ],
        compiler_params=pltpu.CompilerParams(
            collective_id=0, has_side_effects=True, vmem_limit_bytes=48 * 1024 * 1024
        ),
    )(spectra, ids, table)


def solution(mesh):
    in_specs = (P(None, "seg", "chan", None), P("chan", None, None))
    out_specs = P("chan", "seg")
    return jax.shard_map(
        on_device, mesh=mesh, in_specs=in_specs, out_specs=out_specs, check_vma=False
    )
```

```python
import functools
import math

import jax
import jax.numpy as jnp
import numpy as np
from jax import lax
from jax.experimental import pallas as pl
from jax.experimental.pallas import tpu as pltpu
from jax.sharding import PartitionSpec as P

LAGS = 256
NFFT = 1024
LOW_BIN = 16
BIN_WIDTH = 4
REACH = 3
BIN_DEV = 2

MESH = pl.DeviceIdType.MESH
RING = 8
ROWS = 8
COLS = 4
SEGS = 4
SIDES = 2 * SEGS
BLOCK = 32
PANELS = 64
HALO = REACH
CHUNKS = 8
WIDTH = RING // CHUNKS
AHEAD = 2
EARLY = 1
F32 = jnp.float32
BF16 = jnp.bfloat16


def lag_table(freq_count, lag_count):
    bin_index = np.arange(freq_count, dtype=np.int64) + LOW_BIN
    lag_index = np.arange(lag_count, dtype=np.int64) - lag_count // 2
    phase = bin_index[:, None] * lag_index[None, :] % NFFT
    theta = phase.astype(np.float64) * (2.0 * math.pi / NFFT)
    return np.concatenate([np.cos(theta), -np.sin(theta)], axis=0).astype(np.float32)


def split_two(value):
    high = value.astype(BF16)
    return high, (value - high.astype(F32)).astype(BF16)


def fold(values):
    row = lax.broadcasted_iota(jnp.int32, (8, 128), 0)
    upper = row >= 4
    fours = []
    for q in range(4):
        a, b = values[q], values[q + 4]
        fours.append(jnp.where(upper, b, a) + pltpu.roll(jnp.where(upper, a, b), 4, 0))
    upper = lax.rem(row, 4) >= 2
    twos = []
    for q in range(2):
        a, b = fours[q], fours[q + 2]
        twos.append(jnp.where(upper, b + pltpu.roll(b, 2, 0), a + pltpu.roll(a, 6, 0)))
    upper = lax.rem(row, 2) >= 1
    a, b = twos
    return jnp.where(upper, b + pltpu.roll(b, 1, 0), a + pltpu.roll(a, 7, 0))


def kernel(
    norm_factor, x_ref, pb_ref, table_in, o_ref,
    gathered, sources, sums, totals, panels, bins_in, table, a_out, a_in, b_out, b_in, c_out, c_in,
    local_sem, x_send, x_recv, h_send, h_recv, p_send, p_recv, a_send, a_recv, b_send, b_recv, c_send, c_recv,
):
    chan = lax.axis_index("chan")
    seg = lax.axis_index("seg")
    z = lax.rem(chan, RING)
    row = lax.div(chan, RING)
    y = lax.rem(row, COLS)
    upper = lax.div(row, COLS)
    base = chan - z
    side = upper * SEGS + seg

    def ring_peer(d):
        return lax.rem(z + d, RING)

    def y_peer(d):
        return lax.rem(y + d, COLS)

    def side_peer(d):
        return lax.rem(side + d, SIDES)

    def side_device(other):
        return ((lax.div(other, SEGS) * COLS + y) * RING + z, lax.rem(other, SEGS))

    def y_device(other):
        return ((upper * COLS + other) * RING + z, seg)

    next_row = (lax.rem(row + 1, ROWS) * RING + z, seg)
    prev_row = (lax.rem(row + ROWS - 1, ROWS) * RING + z, seg)
    has_next = row < ROWS - 1
    has_prev = row > 0

    barrier = pltpu.get_barrier_semaphore()

    def greet(device):
        pl.semaphore_signal(barrier, inc=1, device_id=device, device_id_type=MESH)

    for d in range(1, RING):
        greet((base + ring_peer(d), seg))
    greet(next_row)
    greet(prev_row)
    for d in range(1, COLS):
        greet(y_device(y_peer(d)))
    for d in range(1, SIDES):
        greet(side_device(side_peer(d)))

    own = pltpu.make_async_copy(x_ref.at[:, pl.ds(z * RING, RING)], gathered.at[HALO + z], local_sem.at[0])
    own.start()
    own_bins = pltpu.make_async_copy(pb_ref.at[0], bins_in.at[z], local_sem.at[1])
    own_bins.start()
    own_table = pltpu.make_async_copy(table_in, table, local_sem.at[2])
    own_table.start()
    pl.semaphore_wait(barrier, RING - 1 + 2 + COLS - 1 + SIDES - 1)

    order = [4, 3, 5, 2, 6, 1, 7]

    def block_copy(chunk, d):
        to = ring_peer(d)
        return pltpu.make_async_remote_copy(
            src_ref=x_ref.at[:, pl.ds(to * RING + chunk * WIDTH, WIDTH)],
            dst_ref=gathered.at[HALO + z, :, pl.ds(chunk * WIDTH, WIDTH)],
            send_sem=x_send.at[chunk, d], recv_sem=x_recv.at[chunk, z],
            device_id=(base + to, seg), device_id_type=MESH,
        )

    def block_arrival(chunk, source):
        return pltpu.make_async_remote_copy(
            src_ref=x_ref.at[:, pl.ds(chunk * WIDTH, WIDTH)],
            dst_ref=gathered.at[HALO + source, :, pl.ds(chunk * WIDTH, WIDTH)],
            send_sem=x_send.at[chunk, 0], recv_sem=x_recv.at[chunk, source],
            device_id=(base + ring_peer(1), seg), device_id_type=MESH,
        )

    def halo_copy(chunk):
        return pltpu.make_async_remote_copy(
            src_ref=gathered.at[pl.ds(RING, HALO), :, pl.ds(chunk * WIDTH, WIDTH)],
            dst_ref=gathered.at[pl.ds(0, HALO), :, pl.ds(chunk * WIDTH, WIDTH)],
            send_sem=h_send.at[chunk], recv_sem=h_recv.at[chunk],
            device_id=next_row, device_id_type=MESH,
        )

    def bins_copy(d):
        return pltpu.make_async_remote_copy(
            src_ref=pb_ref.at[0], dst_ref=bins_in.at[z],
            send_sem=p_send.at[d], recv_sem=p_recv.at[d],
            device_id=(base + ring_peer(d), seg), device_id_type=MESH,
        )

    def send_chunk(chunk):
        for d in order:
            block_copy(chunk, d).start()

    first_sent = z >= RING - HALO
    for chunk in range(AHEAD):
        send_chunk(chunk)

    @pl.when(first_sent)
    def _():
        for chunk in range(AHEAD, AHEAD + EARLY):
            send_chunk(chunk)

    for d in order:
        bins_copy(d).start()

    def clear(n, carry):
        totals[n] = jnp.zeros(totals.shape[1:], F32)
        return carry

    lax.fori_loop(0, totals.shape[0], clear, 0)

    @pl.when(jnp.logical_not(has_prev))
    def _():
        gathered[0:HALO] = jnp.zeros((HALO,) + gathered.shape[1:], BF16)

    own.wait()

    def prepare(chunk, n, is_source):
        for w in range(WIDTH):
            for tile in range(2):
                lanes = pl.ds(tile * 128, 128)
                real = gathered[n, 0, chunk * WIDTH + w, :, lanes].astype(F32)
                imag = gathered[n, 1, chunk * WIDTH + w, :, lanes].astype(F32)
                if is_source:
                    sources[n - HALO, w, 0, tile] = real
                    sources[n - HALO, w, 1, tile] = imag
                    sources[n - HALO, w, 2, tile] = real - imag
                parts = []
                for part in (real, imag):
                    padded = jnp.concatenate([jnp.zeros((8, 128), F32), part], axis=0)
                    pairs = padded + pltpu.roll(padded, BLOCK + 8 - 1, 0)
                    parts.append((padded, pairs + pltpu.roll(pairs, BLOCK + 8 - 2, 0)))
                (real_pad, real_sum), (imag_pad, imag_sum) = parts
                odd_real = pltpu.roll(real_sum, BLOCK + 8 - 4, 0)
                odd_imag = pltpu.roll(imag_sum, BLOCK + 8 - 4, 0)
                sums[n, w, 0, 0, tile] = real_sum
                sums[n, w, 0, 1, tile] = imag_sum
                sums[n, w, 0, 2, tile] = real_sum + imag_sum
                sums[n, w, 1, 0, tile] = odd_real
                sums[n, w, 1, 1, tile] = odd_imag
                sums[n, w, 1, 2, tile] = odd_real + odd_imag
                if is_source:
                    other_real = real_sum - real_pad
                    other_imag = imag_sum - imag_pad
                    sums[n + RING, w, 0, 0, tile] = other_real
                    sums[n + RING, w, 0, 1, tile] = other_imag
                    sums[n + RING, w, 0, 2, tile] = other_real + other_imag

    def correlate(n, last):
        s = lax.div(n, REACH + 1)
        k = lax.rem(n, REACH + 1)
        partner = HALO + s - k
        centre = jnp.where(k == 0, HALO + RING + s, partner)
        for tile in range(2):
            for parity in range(2):
                place = n * 4 + tile * 2 + parity
                acc = [[totals[place, q * 3 + m] for m in range(3)] for q in range(8)]
                for w in range(WIDTH):
                    left = [[sources[s, w, m, tile, 8 * i:8 * i + 8, :] for m in range(3)] for i in range(4)]
                    for j in range(-1, 4):
                        at = slice(8 * j + 8, 8 * j + 16)
                        right = [sums[partner, w, parity, m, tile, at, :] for m in range(3)]
                        for i in range(4):
                            q = j - i + 4
                            if not 0 <= q < 8:
                                continue
                            used = right
                            if parity == 0 and q == 4:
                                used = [sums[centre, w, 0, m, tile, at, :] for m in range(3)]
                            for m in range(3):
                                acc[q][m] = acc[q][m] + left[i][m] * used[m]
                if last:
                    where = pl.ds(n * 16 + parity, 8, stride=2)
                    real = fold([a + b for a, b, c in acc])
                    imag = fold([c - a + b for a, b, c in acc])
                    panels[tile, where, :] = real
                    panels[2 + tile, where, :] = imag
                else:
                    for q in range(8):
                        for m in range(3):
                            totals[place, q * 3 + m] = acc[q][m]

    def loop(start, stop, body):
        def step(n, carry):
            body(n)
            return carry

        lax.fori_loop(start, stop, step, 0)

    def one_chunk(chunk, last):
        for source in range(RING - HALO, RING):
            @pl.when(z != source)
            def _():
                block_arrival(chunk, source).wait_recv()

        @pl.when(has_next)
        def _():
            halo_copy(chunk).start()

        for source in range(RING - HALO):
            @pl.when(z != source)
            def _():
                block_arrival(chunk, source).wait_recv()

        for d in order:
            block_copy(chunk, d).wait_send()
        if not last:
            @pl.when(jnp.logical_not(first_sent) & (chunk + AHEAD < CHUNKS))
            def _():
                send_chunk(chunk + AHEAD)

            @pl.when(first_sent & (chunk + AHEAD + EARLY < CHUNKS))
            def _():
                send_chunk(chunk + AHEAD + EARLY)

        loop(HALO, HALO + RING, lambda n: prepare(chunk, n, True))
        loop(REACH * (REACH + 1), RING * (REACH + 1), lambda n: correlate(n, last))

        @pl.when(has_prev)
        def _():
            halo_copy(chunk).wait_recv()

        loop(0, HALO, lambda n: prepare(chunk, n, False))
        loop(0, REACH * (REACH + 1), lambda n: correlate(n, last))

        @pl.when(has_next)
        def _():
            halo_copy(chunk).wait_send()

    loop(0, CHUNKS - 1, lambda chunk: one_chunk(chunk, False))
    one_chunk(CHUNKS - 1, True)

    for d in order:
        bins_copy(d).wait()
    own_bins.wait()
    own_table.wait()

    index = lax.broadcasted_iota(jnp.int32, (128, PANELS), 0)
    owner = lax.rem(index, 2) * (COLS * RING) + lax.rem(lax.div(index, 4), COLS) * RING + lax.div(index, 16)
    bin_ids = BIN_DEV * owner + lax.rem(lax.div(index, 2), 2)
    binned = jnp.zeros((128, 512), F32)
    for s in range(RING):
        hot = jnp.where(bin_ids == bins_in[s], 1.0, 0.0).astype(BF16)
        rows = slice(s * PANELS, (s + 1) * PANELS)
        for part in split_two(jnp.concatenate([panels[t, rows, :] for t in range(4)], axis=1)):
            binned = binned + jnp.dot(hot, part, preferred_element_type=F32)
    high, low = split_two(binned)
    table_high, table_low = split_two(table[...])
    lagged = (
        jnp.dot(high, table_high, preferred_element_type=F32)
        + jnp.dot(low, table_high, preferred_element_type=F32)
        + jnp.dot(high, table_low, preferred_element_type=F32)
    )
    a_out[...] = lagged.reshape(RING, 16, LAGS)

    def a_copy(d):
        to = ring_peer(d)
        return pltpu.make_async_remote_copy(
            src_ref=a_out.at[to], dst_ref=a_in.at[z], send_sem=a_send.at[d], recv_sem=a_recv.at[d],
            device_id=(base + to, seg), device_id_type=MESH,
        )

    def b_copy(d):
        to = y_peer(d)
        return pltpu.make_async_remote_copy(
            src_ref=b_out.at[to], dst_ref=b_in.at[y], send_sem=b_send.at[d], recv_sem=b_recv.at[d],
            device_id=y_device(to), device_id_type=MESH,
        )

    def c_copy(d):
        to = side_peer(d)
        return pltpu.make_async_remote_copy(
            src_ref=c_out.at[to], dst_ref=c_in.at[side], send_sem=c_send.at[d], recv_sem=c_recv.at[d],
            device_id=side_device(to), device_id_type=MESH,
        )

    for d in order:
        a_copy(d).start()
    total = a_out[z]
    for d in order:
        a_copy(d).wait_recv()
    for d in range(1, RING):
        total = total + a_in[ring_peer(d)]
    for r in range(COLS):
        b_out[r] = total[4 * r:4 * r + 4, :]
    for d in range(1, COLS):
        b_copy(d).start()
    total = b_out[y]
    for d in range(1, COLS):
        b_copy(d).wait_recv()
    for d in range(1, COLS):
        total = total + b_in[y_peer(d)]
    for g in range(SEGS):
        both = jnp.concatenate([total[0:2, g * 64:g * 64 + 64], total[2:4, g * 64:g * 64 + 64]], axis=1)
        for r in range(2):
            c_out[r * SEGS + g] = both[r:r + 1, :]
    for d in range(1, SIDES):
        c_copy(d).start()
    result = c_out[side]
    for d in range(1, SIDES):
        c_copy(d).wait_recv()
    for d in range(1, SIDES):
        result = result + c_in[side_peer(d)]
    result = result * norm_factor
    o_ref[0:1, :] = result[:, 0:64]
    o_ref[1:2, :] = result[:, 64:128]
    for d in order:
        a_copy(d).wait_send()
    for d in range(1, COLS):
        b_copy(d).wait_send()
    for d in range(1, SIDES):
        c_copy(d).wait_send()


def on_device(spectra, pair_bins):
    window_count = spectra.shape[1]
    freq_count = spectra.shape[3]
    panel_count = pair_bins.shape[1]
    norm_factor = 1.0 / math.sqrt(
        window_count * SEGS * BLOCK * BIN_WIDTH * freq_count * panel_count / BIN_DEV
    )
    table = jnp.asarray(lag_table(freq_count, LAGS))
    vmem = pl.BlockSpec(memory_space=pltpu.VMEM)
    anywhere = pl.BlockSpec(memory_space=pl.ANY)
    dma = pltpu.SemaphoreType.DMA
    return pl.pallas_call(
        functools.partial(kernel, norm_factor),
        out_shape=jax.ShapeDtypeStruct((BIN_DEV, LAGS // SEGS), F32),
        in_specs=[anywhere, anywhere, anywhere],
        out_specs=vmem,
        scratch_shapes=[
            pltpu.VMEM((HALO + RING, 2, RING, BLOCK, 256), BF16),
            pltpu.VMEM((RING, WIDTH, 3, 2, BLOCK, 128), F32),
            pltpu.VMEM((HALO + 2 * RING, WIDTH, 2, 3, 2, BLOCK + 8, 128), F32),
            pltpu.VMEM((RING * (REACH + 1) * 4, 24, 8, 128), F32),
            pltpu.VMEM((4, RING * PANELS, 128), F32),
            pltpu.VMEM((RING, 1, PANELS), jnp.int32),
            pltpu.VMEM((2 * 256, LAGS), F32),
            pltpu.VMEM((RING, 16, LAGS), F32),
            pltpu.VMEM((RING, 16, LAGS), F32),
            pltpu.VMEM((COLS, 4, LAGS), F32),
            pltpu.VMEM((COLS, 4, LAGS), F32),
            pltpu.VMEM((SIDES, 1, 128), F32),
            pltpu.VMEM((SIDES, 1, 128), F32),
            dma((3,)),
            dma((CHUNKS, RING)), dma((CHUNKS, RING)),
            dma((CHUNKS,)), dma((CHUNKS,)),
            dma((RING,)), dma((RING,)),
            dma((RING,)), dma((RING,)),
            dma((COLS,)), dma((COLS,)),
            dma((SIDES,)), dma((SIDES,)),
        ],
        compiler_params=pltpu.CompilerParams(
            collective_id=0, has_side_effects=True, vmem_limit_bytes=60 * 1024 * 1024
        ),
    )(spectra, pair_bins.transpose(0, 2, 1), table)


def solution(mesh):
    in_specs = (P(None, "seg", "chan", None), P("chan", None, None))
    out_specs = P("chan", "seg")
    return jax.shard_map(
        on_device, mesh=mesh, in_specs=in_specs, out_specs=out_specs, check_vma=False
    )
```

```python
import functools
import math

import jax
import jax.numpy as jnp
import numpy as np
from jax import lax
from jax.experimental import pallas as pl
from jax.experimental.pallas import tpu as pltpu
from jax.sharding import PartitionSpec as P

LAGS = 256
NFFT = 1024
LOW_BIN = 16
BIN_WIDTH = 4
REACH = 3
BIN_DEV = 2

MESH = pl.DeviceIdType.MESH
RING = 8
ROWS = 8
CORES = 2
HALVES = 2
SEGS = HALVES * CORES
PLANE = ROWS * HALVES
COLUMN = RING * CORES
BLOCK = 32
PANELS = 64
HALO = REACH
CHUNKS = 8
WIDTH = RING // CHUNKS
AHEAD = 2
EARLY = 1
F32 = jnp.float32
BF16 = jnp.bfloat16


def lag_table(freq_count, lag_count):
    bin_index = np.arange(freq_count, dtype=np.int64) + LOW_BIN
    lag_index = np.arange(lag_count, dtype=np.int64) - lag_count // 2
    phase = bin_index[:, None] * lag_index[None, :] % NFFT
    theta = phase.astype(np.float64) * (2.0 * math.pi / NFFT)
    return np.concatenate([np.cos(theta), -np.sin(theta)], axis=0).astype(np.float32)


def split_two(value):
    high = value.astype(BF16)
    return high, (value - high.astype(F32)).astype(BF16)


def fold(values):
    row = lax.broadcasted_iota(jnp.int32, (8, 128), 0)
    upper = row >= 4
    fours = []
    for q in range(4):
        a, b = values[q], values[q + 4]
        fours.append(jnp.where(upper, b, a) + pltpu.roll(jnp.where(upper, a, b), 4, 0))
    upper = lax.rem(row, 4) >= 2
    twos = []
    for q in range(2):
        a, b = fours[q], fours[q + 2]
        twos.append(jnp.where(upper, b + pltpu.roll(b, 2, 0), a + pltpu.roll(a, 6, 0)))
    upper = lax.rem(row, 2) >= 1
    a, b = twos
    return jnp.where(upper, b + pltpu.roll(b, 1, 0), a + pltpu.roll(a, 7, 0))


def kernel(
    norm_factor, x_ref, pb_ref, table_in, o_ref,
    gathered, sources, sums, totals, panels, bins_in, table, tables, hot, a_out, a_in, b_out, b_in,
    local_sem, x_send, x_recv, h_send, h_recv, p_send, p_recv, a_send, a_recv, b_send, b_recv,
):
    chan = lax.axis_index("chan")
    seg = lax.axis_index("seg")
    z = lax.rem(chan, RING)
    row = lax.div(chan, RING)
    base = chan - z
    half = lax.div(seg, CORES)
    core = lax.rem(seg, CORES)
    plane = row * HALVES + half
    column = z * CORES + core

    def ring_peer(d):
        return lax.rem(z + d, RING)

    def plane_peer(d):
        return lax.rem(plane + d, PLANE)

    def plane_device(other):
        return (lax.div(other, HALVES) * RING + z, lax.rem(other, HALVES) * CORES + core)

    def column_peer(d):
        return lax.rem(column + d, COLUMN)

    def column_device(other):
        return (base + lax.div(other, CORES), half * CORES + lax.rem(other, CORES))

    next_row = (lax.rem(row + 1, ROWS) * RING + z, seg)
    prev_row = (lax.rem(row + ROWS - 1, ROWS) * RING + z, seg)
    has_next = row < ROWS - 1
    has_prev = row > 0

    barrier = pltpu.get_barrier_semaphore()

    def greet(device):
        pl.semaphore_signal(barrier, inc=1, device_id=device, device_id_type=MESH)

    for d in range(1, COLUMN):
        greet(column_device(column_peer(d)))
    greet(next_row)
    greet(prev_row)
    for d in range(1, PLANE):
        greet(plane_device(plane_peer(d)))

    own = pltpu.make_async_copy(x_ref.at[:, pl.ds(z * RING, RING)], gathered.at[HALO + z], local_sem.at[0])
    own.start()
    own_bins = pltpu.make_async_copy(pb_ref.at[0], bins_in.at[z], local_sem.at[1])
    own_bins.start()
    own_table = pltpu.make_async_copy(table_in, table, local_sem.at[2])
    own_table.start()
    pl.semaphore_wait(barrier, COLUMN - 1 + 2 + PLANE - 1)

    order = [4, 3, 5, 2, 6, 1, 7]

    def block_copy(chunk, d):
        to = ring_peer(d)
        return pltpu.make_async_remote_copy(
            src_ref=x_ref.at[:, pl.ds(to * RING + chunk * WIDTH, WIDTH)],
            dst_ref=gathered.at[HALO + z, :, pl.ds(chunk * WIDTH, WIDTH)],
            send_sem=x_send.at[chunk, d], recv_sem=x_recv.at[chunk, z],
            device_id=(base + to, seg), device_id_type=MESH,
        )

    def block_arrival(chunk, source):
        return pltpu.make_async_remote_copy(
            src_ref=x_ref.at[:, pl.ds(chunk * WIDTH, WIDTH)],
            dst_ref=gathered.at[HALO + source, :, pl.ds(chunk * WIDTH, WIDTH)],
            send_sem=x_send.at[chunk, 0], recv_sem=x_recv.at[chunk, source],
            device_id=(base + ring_peer(1), seg), device_id_type=MESH,
        )

    def halo_copy(chunk):
        return pltpu.make_async_remote_copy(
            src_ref=gathered.at[pl.ds(RING, HALO), :, pl.ds(chunk * WIDTH, WIDTH)],
            dst_ref=gathered.at[pl.ds(0, HALO), :, pl.ds(chunk * WIDTH, WIDTH)],
            send_sem=h_send.at[chunk], recv_sem=h_recv.at[chunk],
            device_id=next_row, device_id_type=MESH,
        )

    def bins_copy(d):
        return pltpu.make_async_remote_copy(
            src_ref=pb_ref.at[0], dst_ref=bins_in.at[z],
            send_sem=p_send.at[d], recv_sem=p_recv.at[d],
            device_id=(base + ring_peer(d), seg), device_id_type=MESH,
        )

    def send_chunk(chunk):
        for d in order:
            block_copy(chunk, d).start()

    first_sent = z >= RING - HALO
    for chunk in range(AHEAD):
        send_chunk(chunk)

    @pl.when(first_sent)
    def _():
        for chunk in range(AHEAD, AHEAD + EARLY):
            send_chunk(chunk)

    for d in order:
        bins_copy(d).start()

    def clear(n, carry):
        totals[n] = jnp.zeros(totals.shape[1:], F32)
        return carry

    lax.fori_loop(0, totals.shape[0], clear, 0)

    @pl.when(jnp.logical_not(has_prev))
    def _():
        gathered[0:HALO] = jnp.zeros((HALO,) + gathered.shape[1:], BF16)

    own.wait()

    def prepare(chunk, n, is_source):
        for w in range(WIDTH):
            for tile in range(2):
                lanes = pl.ds(tile * 128, 128)
                real = gathered[n, 0, chunk * WIDTH + w, :, lanes].astype(F32)
                imag = gathered[n, 1, chunk * WIDTH + w, :, lanes].astype(F32)
                if is_source:
                    sources[n - HALO, w, 0, tile] = real
                    sources[n - HALO, w, 1, tile] = imag
                    sources[n - HALO, w, 2, tile] = real - imag
                parts = []
                for part in (real, imag):
                    padded = jnp.concatenate([jnp.zeros((8, 128), F32), part], axis=0)
                    pairs = padded + pltpu.roll(padded, BLOCK + 8 - 1, 0)
                    parts.append((padded, pairs + pltpu.roll(pairs, BLOCK + 8 - 2, 0)))
                (real_pad, real_sum), (imag_pad, imag_sum) = parts
                odd_real = pltpu.roll(real_sum, BLOCK + 8 - 4, 0)
                odd_imag = pltpu.roll(imag_sum, BLOCK + 8 - 4, 0)
                sums[n, w, 0, 0, tile] = real_sum
                sums[n, w, 0, 1, tile] = imag_sum
                sums[n, w, 0, 2, tile] = real_sum + imag_sum
                sums[n, w, 1, 0, tile] = odd_real
                sums[n, w, 1, 1, tile] = odd_imag
                sums[n, w, 1, 2, tile] = odd_real + odd_imag
                if is_source:
                    other_real = real_sum - real_pad
                    other_imag = imag_sum - imag_pad
                    sums[n + RING, w, 0, 0, tile] = other_real
                    sums[n + RING, w, 0, 1, tile] = other_imag
                    sums[n + RING, w, 0, 2, tile] = other_real + other_imag

    def correlate(n, last):
        s = lax.div(n, REACH + 1)
        k = lax.rem(n, REACH + 1)
        partner = HALO + s - k
        centre = jnp.where(k == 0, HALO + RING + s, partner)
        for tile in range(2):
            for parity in range(2):
                place = n * 4 + tile * 2 + parity
                acc = [[totals[place, q * 3 + m] for m in range(3)] for q in range(8)]
                for w in range(WIDTH):
                    left = [[sources[s, w, m, tile, 8 * i:8 * i + 8, :] for m in range(3)] for i in range(4)]
                    for j in range(-1, 4):
                        at = slice(8 * j + 8, 8 * j + 16)
                        right = [sums[partner, w, parity, m, tile, at, :] for m in range(3)]
                        for i in range(4):
                            q = j - i + 4
                            if not 0 <= q < 8:
                                continue
                            used = right
                            if parity == 0 and q == 4:
                                used = [sums[centre, w, 0, m, tile, at, :] for m in range(3)]
                            for m in range(3):
                                acc[q][m] = acc[q][m] + left[i][m] * used[m]
                if last:
                    where = pl.ds(n * 16 + parity, 8, stride=2)
                    real = fold([a + b for a, b, c in acc])
                    imag = fold([c - a + b for a, b, c in acc])
                    panels[tile, where, :] = real
                    panels[2 + tile, where, :] = imag
                else:
                    for q in range(8):
                        for m in range(3):
                            totals[place, q * 3 + m] = acc[q][m]

    def loop(start, stop, body):
        def step(n, carry):
            body(n)
            return carry

        lax.fori_loop(start, stop, step, 0)

    def inside(i):
        s = (i >= 1).astype(jnp.int32) + (i >= 3).astype(jnp.int32)
        return s * (REACH + 1) + i - lax.div(s * (s + 1), 2)

    def across(i):
        s = (i >= 3).astype(jnp.int32) + (i >= 5).astype(jnp.int32)
        return s * (REACH + 1) + i + 1 - jnp.where(s == 0, 0, s + 1)

    def sum_bins(part):
        rows = slice(part * 256, part * 256 + 256)
        high, low = split_two(jnp.concatenate([panels[t, rows, :] for t in range(4)], axis=1))
        which = hot[:, rows]
        return jnp.dot(which, high, preferred_element_type=F32) + jnp.dot(which, low, preferred_element_type=F32)

    def one_chunk(chunk, last):
        for source in range(RING - HALO, RING):
            @pl.when(z != source)
            def _():
                block_arrival(chunk, source).wait_recv()

        @pl.when(has_next)
        def _():
            halo_copy(chunk).start()

        for source in range(RING - HALO):
            @pl.when(z != source)
            def _():
                block_arrival(chunk, source).wait_recv()

        for d in order:
            block_copy(chunk, d).wait_send()
        if not last:
            @pl.when(jnp.logical_not(first_sent) & (chunk + AHEAD < CHUNKS))
            def _():
                send_chunk(chunk + AHEAD)

            @pl.when(first_sent & (chunk + AHEAD + EARLY < CHUNKS))
            def _():
                send_chunk(chunk + AHEAD + EARLY)

        loop(HALO, HALO + RING, lambda n: prepare(chunk, n, True))
        loop(REACH * (REACH + 1), RING * (REACH + 1), lambda n: correlate(n, last))
        loop(0, 6, lambda i: correlate(inside(i), last))
        if last:
            binned = sum_bins(1)

        @pl.when(has_prev)
        def _():
            halo_copy(chunk).wait_recv()

        loop(0, HALO, lambda n: prepare(chunk, n, False))
        loop(0, 6, lambda i: correlate(across(i), last))
        if last:
            binned = binned + sum_bins(0)

        @pl.when(has_next)
        def _():
            halo_copy(chunk).wait_send()

        return binned if last else None

    def many_chunks(chunk):
        one_chunk(chunk, False)

    loop(0, CHUNKS - 1, many_chunks)

    for d in order:
        bins_copy(d).wait()
    own_bins.wait()
    own_table.wait()

    index = lax.broadcasted_iota(jnp.int32, (128, PANELS), 0)
    bin_ids = BIN_DEV * (lax.div(index, 16) * RING + lax.rem(index, 8)) + lax.rem(lax.div(index, 8), 2)
    for s in range(0, RING, 2):
        pair = [jnp.where(bin_ids == bins_in[s + i], 1.0, 0.0) for i in range(2)]
        hot[:, s * PANELS:(s + 2) * PANELS] = jnp.concatenate(pair, axis=1).astype(BF16)
    tables[0], tables[1] = split_two(table[...])

    binned = one_chunk(CHUNKS - 1, True)
    high, low = split_two(binned)
    both = jnp.dot(jnp.concatenate([high, low], axis=0), tables[0], preferred_element_type=F32)
    lagged = both[0:128] + both[128:256] + jnp.dot(high, tables[1], preferred_element_type=F32)
    for h in range(HALVES):
        a_out[:, h] = lagged[:, h * 128:h * 128 + 128].reshape(ROWS, 16, 128)

    def a_copy(d):
        to = plane_peer(d)
        return pltpu.make_async_remote_copy(
            src_ref=a_out.at[lax.div(to, HALVES), lax.rem(to, HALVES)], dst_ref=a_in.at[plane],
            send_sem=a_send.at[d], recv_sem=a_recv.at[d],
            device_id=plane_device(to), device_id_type=MESH,
        )

    def b_copy(d):
        to = column_peer(d)
        return pltpu.make_async_remote_copy(
            src_ref=b_out.at[to], dst_ref=b_in.at[column], send_sem=b_send.at[d], recv_sem=b_recv.at[d],
            device_id=column_device(to), device_id_type=MESH,
        )

    for d in range(1, PLANE):
        a_copy(d).start()
    total = a_out[row, half]
    for d in range(1, PLANE):
        a_copy(d).wait_recv()
    for d in range(1, PLANE):
        total = total + a_in[plane_peer(d)]
    for c in range(CORES):
        both = jnp.concatenate([total[0:8, c * 64:c * 64 + 64], total[8:16, c * 64:c * 64 + 64]], axis=1)
        for r in range(RING):
            b_out[r * CORES + c] = both[r:r + 1, :]
    for d in range(1, COLUMN):
        b_copy(d).start()
    result = b_out[column]
    for d in range(1, COLUMN):
        b_copy(d).wait_recv()
    for d in range(1, COLUMN):
        result = result + b_in[column_peer(d)]
    result = result * norm_factor
    o_ref[0:1, :] = result[:, 0:64]
    o_ref[1:2, :] = result[:, 64:128]
    for d in range(1, PLANE):
        a_copy(d).wait_send()
    for d in range(1, COLUMN):
        b_copy(d).wait_send()


def on_device(spectra, pair_bins):
    window_count = spectra.shape[1]
    freq_count = spectra.shape[3]
    panel_count = pair_bins.shape[1]
    norm_factor = 1.0 / math.sqrt(
        window_count * SEGS * BLOCK * BIN_WIDTH * freq_count * panel_count / BIN_DEV
    )
    table = jnp.asarray(lag_table(freq_count, LAGS))
    vmem = pl.BlockSpec(memory_space=pltpu.VMEM)
    anywhere = pl.BlockSpec(memory_space=pl.ANY)
    dma = pltpu.SemaphoreType.DMA
    return pl.pallas_call(
        functools.partial(kernel, norm_factor),
        out_shape=jax.ShapeDtypeStruct((BIN_DEV, LAGS // SEGS), F32),
        in_specs=[anywhere, anywhere, anywhere],
        out_specs=vmem,
        scratch_shapes=[
            pltpu.VMEM((HALO + RING, 2, RING, BLOCK, 256), BF16),
            pltpu.VMEM((RING, WIDTH, 3, 2, BLOCK, 128), F32),
            pltpu.VMEM((HALO + 2 * RING, WIDTH, 2, 3, 2, BLOCK + 8, 128), F32),
            pltpu.VMEM((RING * (REACH + 1) * 4, 24, 8, 128), F32),
            pltpu.VMEM((4, RING * PANELS, 128), F32),
            pltpu.VMEM((RING, 1, PANELS), jnp.int32),
            pltpu.VMEM((2 * 256, LAGS), F32),
            pltpu.VMEM((2, 2 * 256, LAGS), BF16),
            pltpu.VMEM((128, RING * PANELS), BF16),
            pltpu.VMEM((ROWS, HALVES, 16, 128), F32),
            pltpu.VMEM((PLANE, 16, 128), F32),
            pltpu.VMEM((COLUMN, 1, 128), F32),
            pltpu.VMEM((COLUMN, 1, 128), F32),
            dma((3,)),
            dma((CHUNKS, RING)), dma((CHUNKS, RING)),
            dma((CHUNKS,)), dma((CHUNKS,)),
            dma((RING,)), dma((RING,)),
            dma((PLANE,)), dma((PLANE,)),
            dma((COLUMN,)), dma((COLUMN,)),
        ],
        compiler_params=pltpu.CompilerParams(
            collective_id=0, has_side_effects=True, vmem_limit_bytes=60 * 1024 * 1024
        ),
    )(spectra, pair_bins.transpose(0, 2, 1), table)


def solution(mesh):
    in_specs = (P(None, "seg", "chan", None), P("chan", None, None))
    out_specs = P("chan", "seg")
    return jax.shard_map(
        on_device, mesh=mesh, in_specs=in_specs, out_specs=out_specs, check_vma=False
    )
```

```python
import functools
import math

import jax
import jax.numpy as jnp
import numpy as np
from jax import lax
from jax.experimental import pallas as pl
from jax.experimental.pallas import tpu as pltpu
from jax.sharding import PartitionSpec as P

LAGS = 256
NFFT = 1024
LOW_BIN = 16
BIN_WIDTH = 4
REACH = 3
BIN_DEV = 2

MESH = pl.DeviceIdType.MESH
RING = 8
ROWS = 8
CORES = 2
HALVES = 2
SEGS = HALVES * CORES
PLANE = ROWS * HALVES
COLUMN = RING * CORES
BLOCK = 32
PANELS = 64
HALO = REACH
CHUNKS = 8
WIDTH = RING // CHUNKS
AHEAD = 2
F32 = jnp.float32
BF16 = jnp.bfloat16


def lag_table(freq_count, lag_count):
    bin_index = np.arange(freq_count, dtype=np.int64) + LOW_BIN
    lag_index = np.arange(lag_count, dtype=np.int64) - lag_count // 2
    phase = bin_index[:, None] * lag_index[None, :] % NFFT
    theta = phase.astype(np.float64) * (2.0 * math.pi / NFFT)
    return np.concatenate([np.cos(theta), -np.sin(theta)], axis=0).astype(np.float32)


def split_two(value):
    high = value.astype(BF16)
    return high, (value - high.astype(F32)).astype(BF16)


def far_first(count):
    return sorted(range(1, count), key=lambda d: -min(d, count - d))


def fold(values):
    row = lax.broadcasted_iota(jnp.int32, (8, 128), 0)
    upper = row >= 4
    fours = []
    for q in range(4):
        a, b = values[q], values[q + 4]
        fours.append(jnp.where(upper, b, a) + pltpu.roll(jnp.where(upper, a, b), 4, 0))
    upper = lax.rem(row, 4) >= 2
    twos = []
    for q in range(2):
        a, b = fours[q], fours[q + 2]
        twos.append(jnp.where(upper, b + pltpu.roll(b, 2, 0), a + pltpu.roll(a, 6, 0)))
    upper = lax.rem(row, 2) >= 1
    a, b = twos
    return jnp.where(upper, b + pltpu.roll(b, 1, 0), a + pltpu.roll(a, 7, 0))


def kernel(
    norm_factor, x_ref, pb_ref, table_in, o_ref,
    gathered, sources, sums, totals, panels, bins_in, table, tables, hot, a_out, a_in, b_out, b_in,
    local_sem, x_send, x_recv, h_send, h_recv, p_send, p_recv, a_send, a_recv, b_send, b_recv,
):
    chan = lax.axis_index("chan")
    seg = lax.axis_index("seg")
    z = lax.rem(chan, RING)
    row = lax.div(chan, RING)
    base = chan - z
    half = lax.div(seg, CORES)
    core = lax.rem(seg, CORES)
    plane = row * HALVES + half
    column = z * CORES + core

    def ring_peer(d):
        return lax.rem(z + d, RING)

    def plane_peer(d):
        return lax.rem(plane + d, PLANE)

    def plane_device(other):
        return (lax.div(other, HALVES) * RING + z, lax.rem(other, HALVES) * CORES + core)

    def column_peer(d):
        return lax.rem(column + d, COLUMN)

    def column_device(other):
        return (base + lax.div(other, CORES), half * CORES + lax.rem(other, CORES))

    next_row = (lax.rem(row + 1, ROWS) * RING + z, seg)
    prev_row = (lax.rem(row + ROWS - 1, ROWS) * RING + z, seg)
    has_next = row < ROWS - 1
    has_prev = row > 0

    barrier = pltpu.get_barrier_semaphore()

    def greet(device):
        pl.semaphore_signal(barrier, inc=1, device_id=device, device_id_type=MESH)

    for d in far_first(COLUMN):
        greet(column_device(column_peer(d)))
    greet(next_row)
    greet(prev_row)
    for d in range(1, PLANE):
        greet(plane_device(plane_peer(d)))

    own = pltpu.make_async_copy(x_ref.at[:, pl.ds(z * RING, RING)], gathered.at[HALO + z], local_sem.at[0])
    own.start()
    own_bins = pltpu.make_async_copy(pb_ref.at[0], bins_in.at[z], local_sem.at[1])
    own_bins.start()
    own_table = pltpu.make_async_copy(table_in, table, local_sem.at[2])
    own_table.start()
    pl.semaphore_wait(barrier, COLUMN - 1 + 2 + PLANE - 1)

    order = [4, 3, 5, 2, 6, 1, 7]

    def block_copy(chunk, d):
        to = ring_peer(d)
        return pltpu.make_async_remote_copy(
            src_ref=x_ref.at[:, pl.ds(to * RING + chunk * WIDTH, WIDTH)],
            dst_ref=gathered.at[HALO + z, :, pl.ds(chunk * WIDTH, WIDTH)],
            send_sem=x_send.at[chunk, d], recv_sem=x_recv.at[chunk, z],
            device_id=(base + to, seg), device_id_type=MESH,
        )

    def block_arrival(chunk, source):
        return pltpu.make_async_remote_copy(
            src_ref=x_ref.at[:, pl.ds(chunk * WIDTH, WIDTH)],
            dst_ref=gathered.at[HALO + source, :, pl.ds(chunk * WIDTH, WIDTH)],
            send_sem=x_send.at[chunk, 0], recv_sem=x_recv.at[chunk, source],
            device_id=(base + ring_peer(1), seg), device_id_type=MESH,
        )

    def halo_copy(chunk, block):
        return pltpu.make_async_remote_copy(
            src_ref=gathered.at[RING + block, :, pl.ds(chunk * WIDTH, WIDTH)],
            dst_ref=gathered.at[block, :, pl.ds(chunk * WIDTH, WIDTH)],
            send_sem=h_send.at[chunk, block], recv_sem=h_recv.at[chunk, block],
            device_id=next_row, device_id_type=MESH,
        )

    def bins_copy(d):
        return pltpu.make_async_remote_copy(
            src_ref=pb_ref.at[0], dst_ref=bins_in.at[z],
            send_sem=p_send.at[d], recv_sem=p_recv.at[d],
            device_id=(base + ring_peer(d), seg), device_id_type=MESH,
        )

    def send_chunk(chunk):
        for d in order:
            block_copy(chunk, d).start()

    for chunk in range(AHEAD):
        send_chunk(chunk)

    for d in order:
        bins_copy(d).start()

    def clear(n, carry):
        totals[n] = jnp.zeros(totals.shape[1:], F32)
        return carry

    lax.fori_loop(0, totals.shape[0], clear, 0)

    @pl.when(jnp.logical_not(has_prev))
    def _():
        gathered[0:HALO] = jnp.zeros((HALO,) + gathered.shape[1:], BF16)

    own.wait()

    def prepare(chunk, n, is_source):
        for w in range(WIDTH):
            for tile in range(2):
                lanes = pl.ds(tile * 128, 128)
                real = gathered[n, 0, chunk * WIDTH + w, :, lanes].astype(F32)
                imag = gathered[n, 1, chunk * WIDTH + w, :, lanes].astype(F32)
                if is_source:
                    sources[n - HALO, w, 0, tile] = real
                    sources[n - HALO, w, 1, tile] = imag
                    sources[n - HALO, w, 2, tile] = real - imag
                parts = []
                for part in (real, imag):
                    padded = jnp.concatenate([jnp.zeros((8, 128), F32), part], axis=0)
                    pairs = padded + pltpu.roll(padded, BLOCK + 8 - 1, 0)
                    parts.append((padded, pairs + pltpu.roll(pairs, BLOCK + 8 - 2, 0)))
                (real_pad, real_sum), (imag_pad, imag_sum) = parts
                odd_real = pltpu.roll(real_sum, BLOCK + 8 - 4, 0)
                odd_imag = pltpu.roll(imag_sum, BLOCK + 8 - 4, 0)
                sums[n, w, 0, 0, tile] = real_sum
                sums[n, w, 0, 1, tile] = imag_sum
                sums[n, w, 0, 2, tile] = real_sum + imag_sum
                sums[n, w, 1, 0, tile] = odd_real
                sums[n, w, 1, 1, tile] = odd_imag
                sums[n, w, 1, 2, tile] = odd_real + odd_imag
                if is_source:
                    other_real = real_sum - real_pad
                    other_imag = imag_sum - imag_pad
                    sums[n + RING, w, 0, 0, tile] = other_real
                    sums[n + RING, w, 0, 1, tile] = other_imag
                    sums[n + RING, w, 0, 2, tile] = other_real + other_imag

    def correlate(s, k, same, last):
        n = s * (REACH + 1) + k
        partner = HALO + s - k
        for tile in range(2):
            for w in range(WIDTH):
                left = [[sources[s, w, m, tile, 8 * i:8 * i + 8, :] for m in range(3)] for i in range(4)]
                for parity in range(2):
                    place = n * 4 + tile * 2 + parity
                    acc = [[totals[place, q * 3 + m] for m in range(3)] for q in range(8)]
                    for j in range(-1, 4):
                        at = slice(8 * j + 8, 8 * j + 16)
                        right = [sums[partner, w, parity, m, tile, at, :] for m in range(3)]
                        for i in range(4):
                            q = j - i + 4
                            if not 0 <= q < 8:
                                continue
                            used = right
                            if same and parity == 0 and q == 4:
                                used = [sums[HALO + RING + s, w, 0, m, tile, at, :] for m in range(3)]
                            for m in range(3):
                                acc[q][m] = acc[q][m] + left[i][m] * used[m]
                    if last and w == WIDTH - 1:
                        where = pl.ds(n * 16 + parity, 8, stride=2)
                        panels[tile, where, :] = fold([a + b for a, b, c in acc])
                        panels[2 + tile, where, :] = fold([c - a + b for a, b, c in acc])
                    else:
                        for q in range(8):
                            for m in range(3):
                                totals[place, q * 3 + m] = acc[q][m]

    def loop(start, stop, body, unroll=1):
        def step(n, carry):
            body(n)
            return carry

        lax.fori_loop(start, stop, step, 0, unroll=unroll)

    def earlier(i):
        s = jnp.where(i == 0, 1, 2)
        return s, jnp.where(i == 2, 2, 1)

    def across(i):
        s = (i >= 3).astype(jnp.int32) + (i >= 5).astype(jnp.int32)
        return s, i + 1 - jnp.where(s == 0, 0, s + 1)

    def later(i):
        return HALO + lax.div(i, REACH), 1 + lax.rem(i, REACH)

    def sum_bins(part):
        rows = slice(part * 256, part * 256 + 256)
        high, low = split_two(jnp.concatenate([panels[t, rows, :] for t in range(4)], axis=1))
        which = hot[:, rows]
        return jnp.dot(which, high, preferred_element_type=F32) + jnp.dot(which, low, preferred_element_type=F32)

    def sent(chunk):
        for d in order:
            block_copy(chunk, d).wait_send()

    def halo_sent(chunk):
        @pl.when(has_next)
        def _():
            for block in range(HALO):
                halo_copy(chunk, block).wait_send()

    def forward(chunk):
        for block in range(HALO):
            @pl.when(z != RING - HALO + block)
            def _():
                block_arrival(chunk, RING - HALO + block).wait_recv()

            @pl.when(has_next)
            def _():
                halo_copy(chunk, block).start()

    def one_chunk(chunk, last):
        if not last:
            forward(chunk)

        for source in range(RING - HALO):
            @pl.when(z != source)
            def _():
                block_arrival(chunk, source).wait_recv()

        if not last:
            sent(chunk)

            @pl.when(chunk + AHEAD < CHUNKS)
            def _():
                send_chunk(chunk + AHEAD)

        loop(HALO, HALO + RING, lambda n: prepare(chunk, n, True), 4)
        loop(0, RING, lambda s: correlate(s, 0, True, last), 4)
        loop(0, 15, lambda i: correlate(*later(i), False, last), 5)
        if last:
            binned = sum_bins(1)
        else:
            @pl.when(chunk == CHUNKS - 2)
            def _():
                forward(CHUNKS - 1)

        loop(0, 3, lambda i: correlate(*earlier(i), False, last), 3)

        @pl.when(has_prev)
        def _():
            for block in range(HALO):
                halo_copy(chunk, block).wait_recv()

        loop(0, HALO, lambda n: prepare(chunk, n, False), 3)
        loop(0, 6, lambda i: correlate(*across(i), False, last), 3)
        if last:
            binned = binned + sum_bins(0)
        else:
            halo_sent(chunk)

        return binned if last else None

    def many_chunks(chunk):
        one_chunk(chunk, False)

    loop(0, CHUNKS - 1, many_chunks)

    for d in order:
        bins_copy(d).wait()
    own_bins.wait()
    own_table.wait()

    index = lax.broadcasted_iota(jnp.int32, (128, PANELS), 0)
    bin_ids = BIN_DEV * (lax.div(index, 16) * RING + lax.rem(index, 8)) + lax.rem(lax.div(index, 8), 2)
    for s in range(0, RING, 2):
        pair = [jnp.where(bin_ids == bins_in[s + i], 1.0, 0.0) for i in range(2)]
        hot[:, s * PANELS:(s + 2) * PANELS] = jnp.concatenate(pair, axis=1).astype(BF16)
    tables[0], tables[1] = split_two(table[...])

    binned = one_chunk(CHUNKS - 1, True)
    high, low = split_two(binned)
    both = jnp.dot(jnp.concatenate([high, low], axis=0), tables[0], preferred_element_type=F32)
    lagged = both[0:128] + both[128:256] + jnp.dot(high, tables[1], preferred_element_type=F32)
    for h in range(HALVES):
        a_out[:, h] = lagged[:, h * 128:h * 128 + 128].reshape(ROWS, 16, 128)

    def a_copy(d):
        to = plane_peer(d)
        return pltpu.make_async_remote_copy(
            src_ref=a_out.at[lax.div(to, HALVES), lax.rem(to, HALVES)], dst_ref=a_in.at[plane],
            send_sem=a_send.at[d], recv_sem=a_recv.at[d],
            device_id=plane_device(to), device_id_type=MESH,
        )

    def b_copy(d):
        to = column_peer(d)
        return pltpu.make_async_remote_copy(
            src_ref=b_out.at[to], dst_ref=b_in.at[column], send_sem=b_send.at[d], recv_sem=b_recv.at[d],
            device_id=column_device(to), device_id_type=MESH,
        )

    for d in range(1, PLANE):
        a_copy(d).start()
    total = a_out[row, half]
    for d in range(1, PLANE):
        a_copy(d).wait_recv()
    for d in range(1, PLANE):
        total = total + a_in[plane_peer(d)]
    for c in range(CORES):
        both = jnp.concatenate([total[0:8, c * 64:c * 64 + 64], total[8:16, c * 64:c * 64 + 64]], axis=1)
        for r in range(RING):
            b_out[r * CORES + c] = both[r:r + 1, :]
    for d in far_first(COLUMN):
        b_copy(d).start()
    result = b_out[column]
    for d in range(1, COLUMN):
        b_copy(d).wait_recv()
    for d in range(1, COLUMN):
        result = result + b_in[column_peer(d)]
    result = result * norm_factor
    o_ref[0:1, :] = result[:, 0:64]
    o_ref[1:2, :] = result[:, 64:128]
    sent(CHUNKS - 1)
    halo_sent(CHUNKS - 1)
    for d in range(1, PLANE):
        a_copy(d).wait_send()
    for d in range(1, COLUMN):
        b_copy(d).wait_send()


def on_device(spectra, pair_bins):
    window_count = spectra.shape[1]
    freq_count = spectra.shape[3]
    panel_count = pair_bins.shape[1]
    norm_factor = 1.0 / math.sqrt(
        window_count * SEGS * BLOCK * BIN_WIDTH * freq_count * panel_count / BIN_DEV
    )
    table = jnp.asarray(lag_table(freq_count, LAGS))
    vmem = pl.BlockSpec(memory_space=pltpu.VMEM)
    anywhere = pl.BlockSpec(memory_space=pl.ANY)
    dma = pltpu.SemaphoreType.DMA
    return pl.pallas_call(
        functools.partial(kernel, norm_factor),
        out_shape=jax.ShapeDtypeStruct((BIN_DEV, LAGS // SEGS), F32),
        in_specs=[anywhere, anywhere, anywhere],
        out_specs=vmem,
        scratch_shapes=[
            pltpu.VMEM((HALO + RING, 2, RING, BLOCK, 256), BF16),
            pltpu.VMEM((RING, WIDTH, 3, 2, BLOCK, 128), F32),
            pltpu.VMEM((HALO + 2 * RING, WIDTH, 2, 3, 2, BLOCK + 8, 128), F32),
            pltpu.VMEM((RING * (REACH + 1) * 4, 24, 8, 128), F32),
            pltpu.VMEM((4, RING * PANELS, 128), F32),
            pltpu.VMEM((RING, 1, PANELS), jnp.int32),
            pltpu.VMEM((2 * 256, LAGS), F32),
            pltpu.VMEM((2, 2 * 256, LAGS), BF16),
            pltpu.VMEM((128, RING * PANELS), BF16),
            pltpu.VMEM((ROWS, HALVES, 16, 128), F32),
            pltpu.VMEM((PLANE, 16, 128), F32),
            pltpu.VMEM((COLUMN, 1, 128), F32),
            pltpu.VMEM((COLUMN, 1, 128), F32),
            dma((3,)),
            dma((CHUNKS, RING)), dma((CHUNKS, RING)),
            dma((CHUNKS, HALO)), dma((CHUNKS, HALO)),
            dma((RING,)), dma((RING,)),
            dma((PLANE,)), dma((PLANE,)),
            dma((COLUMN,)), dma((COLUMN,)),
        ],
        compiler_params=pltpu.CompilerParams(
            collective_id=0, has_side_effects=True, vmem_limit_bytes=60 * 1024 * 1024
        ),
    )(spectra, pair_bins.transpose(0, 2, 1), table)


def solution(mesh):
    in_specs = (P(None, "seg", "chan", None), P("chan", None, None))
    out_specs = P("chan", "seg")
    return jax.shard_map(
        on_device, mesh=mesh, in_specs=in_specs, out_specs=out_specs, check_vma=False
    )
```

```python
import functools
import math

import jax
import jax.numpy as jnp
import numpy as np
from jax import lax
from jax.experimental import pallas as pl
from jax.experimental.pallas import tpu as pltpu
from jax.sharding import PartitionSpec as P

LAGS = 256
NFFT = 1024
LOW_BIN = 16
BIN_WIDTH = 4
REACH = 3
BIN_DEV = 2

MESH = pl.DeviceIdType.MESH
RING = 8
ROWS = 8
CORES = 2
HALVES = 2
SEGS = HALVES * CORES
PLANE = ROWS * HALVES
COLUMN = RING * CORES
BLOCK = 32
PANELS = 64
HALO = REACH
CHUNKS = 8
WIDTH = RING // CHUNKS
AHEAD = 3
F32 = jnp.float32
BF16 = jnp.bfloat16


def lag_table(freq_count, lag_count):
    bin_index = np.arange(freq_count, dtype=np.int64) + LOW_BIN
    lag_index = np.arange(lag_count, dtype=np.int64) - lag_count // 2
    phase = bin_index[:, None] * lag_index[None, :] % NFFT
    theta = phase.astype(np.float64) * (2.0 * math.pi / NFFT)
    return np.concatenate([np.cos(theta), -np.sin(theta)], axis=0).astype(np.float32)


def split_two(value):
    high = value.astype(BF16)
    return high, (value - high.astype(F32)).astype(BF16)


def far_first(count):
    return sorted(range(1, count), key=lambda d: -min(d, count - d))


def fold(values):
    row = lax.broadcasted_iota(jnp.int32, (8, 128), 0)
    upper = row >= 4
    fours = []
    for q in range(4):
        a, b = values[q], values[q + 4]
        fours.append(jnp.where(upper, b, a) + pltpu.roll(jnp.where(upper, a, b), 4, 0))
    upper = lax.rem(row, 4) >= 2
    twos = []
    for q in range(2):
        a, b = fours[q], fours[q + 2]
        twos.append(jnp.where(upper, b + pltpu.roll(b, 2, 0), a + pltpu.roll(a, 6, 0)))
    upper = lax.rem(row, 2) >= 1
    a, b = twos
    return jnp.where(upper, b + pltpu.roll(b, 1, 0), a + pltpu.roll(a, 7, 0))


def kernel(
    norm_factor, x_ref, pb_ref, table_in, o_ref,
    gathered, sources, sums, totals, panels, bins_in, table, tables, hot, a_out, a_in, b_out, b_in,
    local_sem, x_send, x_recv, h_send, h_recv, p_send, p_recv, a_send, a_recv, b_send, b_recv,
):
    chan = lax.axis_index("chan")
    seg = lax.axis_index("seg")
    z = lax.rem(chan, RING)
    row = lax.div(chan, RING)
    base = chan - z
    half = lax.div(seg, CORES)
    core = lax.rem(seg, CORES)
    plane = row * HALVES + half
    column = z * CORES + core

    def ring_peer(d):
        return lax.rem(z + d, RING)

    def plane_peer(d):
        return lax.rem(plane + d, PLANE)

    def plane_device(other):
        return (lax.div(other, HALVES) * RING + z, lax.rem(other, HALVES) * CORES + core)

    def column_peer(d):
        return lax.rem(column + d, COLUMN)

    def column_device(other):
        return (base + lax.div(other, CORES), half * CORES + lax.rem(other, CORES))

    next_row = (lax.rem(row + 1, ROWS) * RING + z, seg)
    prev_row = (lax.rem(row + ROWS - 1, ROWS) * RING + z, seg)
    has_next = row < ROWS - 1
    has_prev = row > 0

    barrier = pltpu.get_barrier_semaphore()

    def greet(device):
        pl.semaphore_signal(barrier, inc=1, device_id=device, device_id_type=MESH)

    for d in far_first(COLUMN):
        greet(column_device(column_peer(d)))
    greet(next_row)
    greet(prev_row)
    for d in range(1, PLANE):
        greet(plane_device(plane_peer(d)))

    own = pltpu.make_async_copy(x_ref.at[:, pl.ds(z * RING, RING)], gathered.at[HALO + z], local_sem.at[0])
    own.start()
    own_bins = pltpu.make_async_copy(pb_ref.at[0], bins_in.at[z], local_sem.at[1])
    own_bins.start()
    own_table = pltpu.make_async_copy(table_in, table, local_sem.at[2])
    own_table.start()
    pl.semaphore_wait(barrier, COLUMN - 1 + 2 + PLANE - 1)

    order = [4, 3, 5, 2, 6, 1, 7]

    def block_copy(chunk, d):
        to = ring_peer(d)
        return pltpu.make_async_remote_copy(
            src_ref=x_ref.at[:, pl.ds(to * RING + chunk * WIDTH, WIDTH)],
            dst_ref=gathered.at[HALO + z, :, pl.ds(chunk * WIDTH, WIDTH)],
            send_sem=x_send.at[chunk, d], recv_sem=x_recv.at[chunk, z],
            device_id=(base + to, seg), device_id_type=MESH,
        )

    def block_arrival(chunk, source):
        return pltpu.make_async_remote_copy(
            src_ref=x_ref.at[:, pl.ds(chunk * WIDTH, WIDTH)],
            dst_ref=gathered.at[HALO + source, :, pl.ds(chunk * WIDTH, WIDTH)],
            send_sem=x_send.at[chunk, 0], recv_sem=x_recv.at[chunk, source],
            device_id=(base + ring_peer(1), seg), device_id_type=MESH,
        )

    def halo_copy(chunk, block):
        return pltpu.make_async_remote_copy(
            src_ref=gathered.at[RING + block, :, pl.ds(chunk * WIDTH, WIDTH)],
            dst_ref=gathered.at[block, :, pl.ds(chunk * WIDTH, WIDTH)],
            send_sem=h_send.at[chunk, block], recv_sem=h_recv.at[chunk, block],
            device_id=next_row, device_id_type=MESH,
        )

    def bins_copy(d):
        return pltpu.make_async_remote_copy(
            src_ref=pb_ref.at[0], dst_ref=bins_in.at[z],
            send_sem=p_send.at[d], recv_sem=p_recv.at[d],
            device_id=(base + ring_peer(d), seg), device_id_type=MESH,
        )

    def send_chunk(chunk):
        for d in order:
            block_copy(chunk, d).start()

    for chunk in range(AHEAD):
        send_chunk(chunk)

    for d in order:
        bins_copy(d).start()

    def clear(n, carry):
        totals[n] = jnp.zeros(totals.shape[1:], F32)
        return carry

    lax.fori_loop(0, totals.shape[0], clear, 0)

    @pl.when(jnp.logical_not(has_prev))
    def _():
        gathered[0:HALO] = jnp.zeros((HALO,) + gathered.shape[1:], BF16)

    own.wait()

    def prepare(chunk, n, is_source):
        for w in range(WIDTH):
            for tile in range(2):
                lanes = pl.ds(tile * 128, 128)
                real = gathered[n, 0, chunk * WIDTH + w, :, lanes].astype(F32)
                imag = gathered[n, 1, chunk * WIDTH + w, :, lanes].astype(F32)
                if is_source:
                    sources[n - HALO, w, 0, tile] = real
                    sources[n - HALO, w, 1, tile] = imag
                    sources[n - HALO, w, 2, tile] = real - imag
                parts = []
                for part in (real, imag):
                    padded = jnp.concatenate([jnp.zeros((8, 128), F32), part], axis=0)
                    pairs = padded + pltpu.roll(padded, BLOCK + 8 - 1, 0)
                    parts.append((padded, pairs + pltpu.roll(pairs, BLOCK + 8 - 2, 0)))
                (real_pad, real_sum), (imag_pad, imag_sum) = parts
                odd_real = pltpu.roll(real_sum, BLOCK + 8 - 4, 0)
                odd_imag = pltpu.roll(imag_sum, BLOCK + 8 - 4, 0)
                sums[n, w, 0, 0, tile] = real_sum
                sums[n, w, 0, 1, tile] = imag_sum
                sums[n, w, 0, 2, tile] = real_sum + imag_sum
                sums[n, w, 1, 0, tile] = odd_real
                sums[n, w, 1, 1, tile] = odd_imag
                sums[n, w, 1, 2, tile] = odd_real + odd_imag
                if is_source:
                    other_real = real_sum - real_pad
                    other_imag = imag_sum - imag_pad
                    sums[n + RING, w, 0, 0, tile] = other_real
                    sums[n + RING, w, 0, 1, tile] = other_imag
                    sums[n + RING, w, 0, 2, tile] = other_real + other_imag

    def correlate(s, k, same, last):
        n = s * (REACH + 1) + k
        partner = HALO + s - k
        for tile in range(2):
            for w in range(WIDTH):
                left = [[sources[s, w, m, tile, 8 * i:8 * i + 8, :] for m in range(3)] for i in range(4)]
                for parity in range(2):
                    place = n * 4 + tile * 2 + parity
                    acc = [[totals[place, q * 3 + m] for m in range(3)] for q in range(8)]
                    for j in range(-1, 4):
                        at = slice(8 * j + 8, 8 * j + 16)
                        right = [sums[partner, w, parity, m, tile, at, :] for m in range(3)]
                        for i in range(4):
                            q = j - i + 4
                            if not 0 <= q < 8:
                                continue
                            used = right
                            if same and parity == 0 and q == 4:
                                used = [sums[HALO + RING + s, w, 0, m, tile, at, :] for m in range(3)]
                            for m in range(3):
                                acc[q][m] = acc[q][m] + left[i][m] * used[m]
                    if last and w == WIDTH - 1:
                        where = pl.ds(n * 16 + parity, 8, stride=2)
                        panels[tile, where, :] = fold([a + b for a, b, c in acc])
                        panels[2 + tile, where, :] = fold([c - a + b for a, b, c in acc])
                    else:
                        for q in range(8):
                            for m in range(3):
                                totals[place, q * 3 + m] = acc[q][m]

    def loop(start, stop, body, unroll=1):
        def step(n, carry):
            body(n)
            return carry

        lax.fori_loop(start, stop, step, 0, unroll=unroll)

    def earlier(i):
        s = jnp.where(i == 0, 1, 2)
        return s, jnp.where(i == 2, 2, 1)

    def across(i):
        s = (i >= 3).astype(jnp.int32) + (i >= 5).astype(jnp.int32)
        return s, i + 1 - jnp.where(s == 0, 0, s + 1)

    def later(i):
        return HALO + lax.div(i, REACH), 1 + lax.rem(i, REACH)

    def sum_bins(part):
        rows = slice(part * 256, part * 256 + 256)
        high, low = split_two(jnp.concatenate([panels[t, rows, :] for t in range(4)], axis=1))
        which = hot[:, rows]
        return jnp.dot(which, high, preferred_element_type=F32) + jnp.dot(which, low, preferred_element_type=F32)

    def sent(chunk):
        for d in order:
            block_copy(chunk, d).wait_send()

    def halo_sent(chunk):
        @pl.when(has_next)
        def _():
            for block in range(HALO):
                halo_copy(chunk, block).wait_send()

    def forward(chunk):
        for block in range(HALO):
            @pl.when(z != RING - HALO + block)
            def _():
                block_arrival(chunk, RING - HALO + block).wait_recv()

            @pl.when(has_next)
            def _():
                halo_copy(chunk, block).start()

    def one_chunk(chunk, last):
        if not last:
            forward(chunk)

        for source in range(RING - HALO):
            @pl.when(z != source)
            def _():
                block_arrival(chunk, source).wait_recv()

        if not last:
            sent(chunk)

            @pl.when(chunk + AHEAD < CHUNKS)
            def _():
                send_chunk(chunk + AHEAD)

        loop(HALO, HALO + RING, lambda n: prepare(chunk, n, True), 4)
        loop(0, RING, lambda s: correlate(s, 0, True, last), 4)
        loop(0, 15, lambda i: correlate(*later(i), False, last), 5)
        if last:
            binned = sum_bins(1)
        else:
            @pl.when(chunk == CHUNKS - 2)
            def _():
                forward(CHUNKS - 1)

        loop(0, 3, lambda i: correlate(*earlier(i), False, last), 3)

        @pl.when(has_prev)
        def _():
            for block in range(HALO):
                halo_copy(chunk, block).wait_recv()

        loop(0, HALO, lambda n: prepare(chunk, n, False), 3)
        loop(0, 6, lambda i: correlate(*across(i), False, last), 3)
        if last:
            binned = binned + sum_bins(0)
        else:
            halo_sent(chunk)

        return binned if last else None

    def many_chunks(chunk):
        one_chunk(chunk, False)

    loop(0, CHUNKS - 1, many_chunks)

    for d in order:
        bins_copy(d).wait()
    own_bins.wait()
    own_table.wait()

    index = lax.broadcasted_iota(jnp.int32, (128, PANELS), 0)
    bin_ids = BIN_DEV * (lax.div(index, 16) * RING + lax.rem(index, 8)) + lax.rem(lax.div(index, 8), 2)
    for s in range(0, RING, 2):
        pair = [jnp.where(bin_ids == bins_in[s + i], 1.0, 0.0) for i in range(2)]
        hot[:, s * PANELS:(s + 2) * PANELS] = jnp.concatenate(pair, axis=1).astype(BF16)
    tables[0], tables[1] = split_two(table[...])

    binned = one_chunk(CHUNKS - 1, True)
    high, low = split_two(binned)
    both = jnp.dot(jnp.concatenate([high, low], axis=0), tables[0], preferred_element_type=F32)
    lagged = both[0:128] + both[128:256] + jnp.dot(high, tables[1], preferred_element_type=F32)
    for h in range(HALVES):
        a_out[:, h] = lagged[:, h * 128:h * 128 + 128].reshape(ROWS, 16, 128)

    def a_copy(d):
        to = plane_peer(d)
        return pltpu.make_async_remote_copy(
            src_ref=a_out.at[lax.div(to, HALVES), lax.rem(to, HALVES)], dst_ref=a_in.at[plane],
            send_sem=a_send.at[d], recv_sem=a_recv.at[d],
            device_id=plane_device(to), device_id_type=MESH,
        )

    def b_copy(d):
        to = column_peer(d)
        return pltpu.make_async_remote_copy(
            src_ref=b_out.at[to], dst_ref=b_in.at[column], send_sem=b_send.at[d], recv_sem=b_recv.at[d],
            device_id=column_device(to), device_id_type=MESH,
        )

    for d in range(1, PLANE):
        a_copy(d).start()
    total = a_out[row, half]
    for d in range(1, PLANE):
        a_copy(d).wait_recv()
    for d in range(1, PLANE):
        total = total + a_in[plane_peer(d)]
    for c in range(CORES):
        both = jnp.concatenate([total[0:8, c * 64:c * 64 + 64], total[8:16, c * 64:c * 64 + 64]], axis=1)
        for r in range(RING):
            b_out[r * CORES + c] = both[r:r + 1, :]
    for d in far_first(COLUMN):
        b_copy(d).start()
    result = b_out[column]
    for d in range(1, COLUMN):
        b_copy(d).wait_recv()
    for d in range(1, COLUMN):
        result = result + b_in[column_peer(d)]
    result = result * norm_factor
    o_ref[0:1, :] = result[:, 0:64]
    o_ref[1:2, :] = result[:, 64:128]
    sent(CHUNKS - 1)
    halo_sent(CHUNKS - 1)
    for d in range(1, PLANE):
        a_copy(d).wait_send()
    for d in range(1, COLUMN):
        b_copy(d).wait_send()


def on_device(spectra, pair_bins):
    window_count = spectra.shape[1]
    freq_count = spectra.shape[3]
    panel_count = pair_bins.shape[1]
    norm_factor = 1.0 / math.sqrt(
        window_count * SEGS * BLOCK * BIN_WIDTH * freq_count * panel_count / BIN_DEV
    )
    table = jnp.asarray(lag_table(freq_count, LAGS))
    vmem = pl.BlockSpec(memory_space=pltpu.VMEM)
    anywhere = pl.BlockSpec(memory_space=pl.ANY)
    dma = pltpu.SemaphoreType.DMA
    return pl.pallas_call(
        functools.partial(kernel, norm_factor),
        out_shape=jax.ShapeDtypeStruct((BIN_DEV, LAGS // SEGS), F32),
        in_specs=[anywhere, anywhere, anywhere],
        out_specs=vmem,
        scratch_shapes=[
            pltpu.VMEM((HALO + RING, 2, RING, BLOCK, 256), BF16),
            pltpu.VMEM((RING, WIDTH, 3, 2, BLOCK, 128), F32),
            pltpu.VMEM((HALO + 2 * RING, WIDTH, 2, 3, 2, BLOCK + 8, 128), F32),
            pltpu.VMEM((RING * (REACH + 1) * 4, 24, 8, 128), F32),
            pltpu.VMEM((4, RING * PANELS, 128), F32),
            pltpu.VMEM((RING, 1, PANELS), jnp.int32),
            pltpu.VMEM((2 * 256, LAGS), F32),
            pltpu.VMEM((2, 2 * 256, LAGS), BF16),
            pltpu.VMEM((128, RING * PANELS), BF16),
            pltpu.VMEM((ROWS, HALVES, 16, 128), F32),
            pltpu.VMEM((PLANE, 16, 128), F32),
            pltpu.VMEM((COLUMN, 1, 128), F32),
            pltpu.VMEM((COLUMN, 1, 128), F32),
            dma((3,)),
            dma((CHUNKS, RING)), dma((CHUNKS, RING)),
            dma((CHUNKS, HALO)), dma((CHUNKS, HALO)),
            dma((RING,)), dma((RING,)),
            dma((PLANE,)), dma((PLANE,)),
            dma((COLUMN,)), dma((COLUMN,)),
        ],
        compiler_params=pltpu.CompilerParams(
            collective_id=0, has_side_effects=True, vmem_limit_bytes=60 * 1024 * 1024
        ),
    )(spectra, pair_bins.transpose(0, 2, 1), table)


def solution(mesh):
    in_specs = (P(None, "seg", "chan", None), P("chan", None, None))
    out_specs = P("chan", "seg")
    return jax.shard_map(
        on_device, mesh=mesh, in_specs=in_specs, out_specs=out_specs, check_vma=False
    )
```
